256 devices in a mesh: dp: 8 (over x, z_lo), ctx: 32 (over y, z_hi, core).
Axes of the slice: x: 4, y: 4, z: 8 (z_hi: 4, z_lo: 2; z = z_hi * 2 + z_lo), core: 2. Of those that a mesh axis runs over, the one named last changes fastest.
Arguments:
- queries: bfloat16 [32768, 8192], P(('dp', 'ctx')), may hold values from -16 to 16
- out_grad: bfloat16 [32768, 8192], P(('dp', 'ctx')), may hold values from -6 to 6
- enc_states: bfloat16 [3072, 1024], P(('dp', 'ctx')), may hold values from -8 to 8
- w_key: bfloat16 [1024, 8192], P('dp', 'ctx'), may hold values from -1 to 1
- w_value: bfloat16 [1024, 8192], P('dp', 'ctx'), may hold values from -0.1875 to 0.1875
- dec_segments: int32 [32768], P(('dp', 'ctx')), may hold values from 0 to 3, as said below
- enc_segments: int32 [3072], P(('dp', 'ctx')), may hold values from 0 to 3, as said below
Outputs:
- query_grad: bfloat16 [32768, 8192], P(('dp', 'ctx'))
- enc_grad: bfloat16 [3072, 1024], P(('dp', 'ctx'))
- w_key_grad: float32 [1024, 8192], P('dp', 'ctx')
- w_value_grad: float32 [1024, 8192], P('dp', 'ctx')
The draws below stay inside these ranges and needn't reach their ends.
Inputs may be any that keep to these rules, and one draw needn't show every extreme that they name: `dec_segments`: within each pack the ids never fall along the tokens, and each of the 4 ids has one or more decoder tokens in the pack. `enc_segments`: within each pack the ids never fall along the tokens, and each of the 4 ids has two or more encoder tokens in the pack.
All inputs are finite; a program needn't handle non-finite values.
Results may differ from the reference program's by a relative error of at most 0.019.
Values may be sent and summed in bfloat16 or wider, within the bound.
No kernel may reach another device: no remote copies, remote signals or barrier semaphores. Data moves between devices by JAX's collectives and lax.ppermute only.
A program may use at most 64 MiB of HBM per device.

```python
import math
import jax
import jax.numpy as jnp
from jax import lax

D = 1024
HEADS = 64
HEAD_DIM = 128
SEGS = 4
WIDTH = 8192
DEC_SEQ = 4096
ENC_SEQ = 384
PACKS = 8
DEC = 32768
ENC = 3072
N_DP = 8


def segment_ids(seed_key, length, spacing):
    slot_count = length // spacing
    boundaries = (jax.random.permutation(seed_key, slot_count - 1)[:SEGS - 1] + 1) * spacing
    boundaries = jnp.sort(boundaries.astype(jnp.int32))
    positions = jnp.arange(length, dtype=jnp.int32)
    labels = jnp.sum((positions[:, None] >= boundaries[None, :]).astype(jnp.int32), axis=1)
    return (labels.astype(jnp.int32), boundaries)


def build(base_key):
    dec_keys = jax.random.split(jax.random.fold_in(base_key, 11), PACKS)
    enc_keys = jax.random.split(jax.random.fold_in(base_key, 12), PACKS)
    dec_ids, unused_bounds = jax.vmap(lambda item: segment_ids(item, DEC_SEQ, 1))(dec_keys)
    enc_ids, enc_bounds = jax.vmap(lambda item: segment_ids(item, ENC_SEQ, 2))(enc_keys)
    key_weight = jnp.clip(jax.random.normal(jax.random.fold_in(base_key, 13), (D, WIDTH), jnp.float32) / math.sqrt(D), -0.99, 0.99)
    encoder = jnp.clip(jax.random.normal(jax.random.fold_in(base_key, 14), (PACKS, ENC_SEQ, D), jnp.float32), -6.0, 6.0)
    queries = jnp.clip(0.09 * jax.random.normal(jax.random.fold_in(base_key, 15), (PACKS, DEC_SEQ, WIDTH), jnp.float32), -0.54, 0.54)
    return (queries, encoder, key_weight, dec_ids, enc_ids)


def draw_queries(key, part):
    return build(key)[0].reshape(DEC, WIDTH).astype(jnp.bfloat16)


def draw_enc_states(key, part):
    return build(key)[1].reshape(ENC, D).astype(jnp.bfloat16)


def draw_w_key(key, part):
    return build(key)[2].astype(jnp.bfloat16)


def draw_dec_segments(key, part):
    return build(key)[3].reshape(DEC).astype(jnp.int32)


def draw_enc_segments(key, part):
    return build(key)[4].reshape(ENC).astype(jnp.int32)


def block_scale(rng, shape, shards, least, largest):
    level, own = 1.0, jax.random.fold_in(rng, 6)
    for position, blocks in shards:
        draws = jnp.exp(jax.random.uniform(jax.random.fold_in(own, position), (blocks,), jnp.float32, least / len(shards), largest / len(shards)))
        level = level * jnp.repeat(draws, shape[position] // blocks).reshape([-1 if axis == position else 1 for axis in range(len(shape))])
    return level


def noise(own_key, extent, spread, reach, cuts=(), held_as=jnp.bfloat16):
    level = block_scale(own_key, extent, cuts, -0.22, 0.18) if cuts else 1.0
    values = jax.random.normal(own_key, extent, jnp.float32) * spread * level
    return jnp.minimum(jnp.maximum(values, -reach), reach).astype(held_as)


def setup_inputs(seed: int = 0) -> dict:
    keys = jax.random.split(jax.random.key(seed), 8)
    queries = draw_queries(jax.random.fold_in(keys[7], 71), 0)
    out_grad = noise(keys[1], (DEC, WIDTH), 1.0, 6.0, ((0, 256),))
    enc_states = draw_enc_states(jax.random.fold_in(keys[7], 71), 0)
    w_key = draw_w_key(jax.random.fold_in(keys[7], 71), 0)
    w_value = noise(keys[4], (D, WIDTH), D ** -0.5, 0.1875, ((0, 8), (1, 32)))
    dec_segments = draw_dec_segments(jax.random.fold_in(keys[7], 71), 0)
    enc_segments = draw_enc_segments(jax.random.fold_in(keys[7], 71), 0)
    return {"queries": queries, "out_grad": out_grad, "enc_states": enc_states, "w_key": w_key, "w_value": w_value, "dec_segments": dec_segments, "enc_segments": enc_segments}


def pack_grads(queries, out_grads, key_rows, value_rows, query_ids, key_ids):
    length = queries.shape[0]
    key_count = key_rows.shape[0]
    group_size = 4 if HEADS % 4 == 0 else 1
    column_count = group_size * HEAD_DIM
    allowed = query_ids[:, None] == key_ids[None, :]

    def head_group(number):
        column_start = number * column_count

        def slice_heads(source, count):
            piece = lax.dynamic_slice_in_dim(source, column_start, column_count, 1)
            return piece.reshape(count, group_size, HEAD_DIM).astype(jnp.float32)

        query_block = slice_heads(queries, length)
        grad_block = slice_heads(out_grads, length)
        key_block = slice_heads(key_rows, key_count)
        value_block = slice_heads(value_rows, key_count)
        scores = jnp.einsum("qhd,khd->hqk", query_block, key_block)
        scores = jnp.where(allowed[None], scores, -jnp.inf)
        highest = jnp.max(scores, axis=2, keepdims=True)
        weights = jnp.exp(scores - highest)
        probability = weights / jnp.sum(weights, axis=2, keepdims=True)
        rounded = lax.optimization_barrier(probability.astype(jnp.bfloat16)).astype(jnp.float32)
        upstream = jnp.einsum("qhd,khd->hqk", grad_block, value_block)
        row_dot = jnp.sum(probability * upstream, axis=2, keepdims=True)
        score_grad = lax.optimization_barrier((probability * (upstream - row_dot)).astype(jnp.bfloat16)).astype(jnp.float32)
        query_grad = jnp.einsum("hqk,khd->qhd", score_grad, key_block).astype(jnp.bfloat16)
        key_grad = jnp.einsum("hqk,qhd->khd", score_grad, query_block)
        value_grad = jnp.einsum("hqk,qhd->khd", rounded, grad_block)
        return (query_grad.reshape(length, column_count), key_grad.reshape(key_count, column_count), value_grad.reshape(key_count, column_count))

    pieces = lax.map(head_group, jnp.arange(HEADS // group_size, dtype=jnp.int32))
    return tuple(jnp.moveaxis(piece, 0, 1).reshape(piece.shape[1], HEADS * HEAD_DIM) for piece in pieces)


def reference(queries, out_grad, enc_states, w_key, w_value, dec_segments, enc_segments):
    full_width = HEADS * HEAD_DIM
    key_all = jnp.dot(enc_states, w_key, preferred_element_type=jnp.float32).astype(jnp.bfloat16)
    value_all = jnp.dot(enc_states, w_value, preferred_element_type=jnp.float32).astype(jnp.bfloat16)
    stacked = (queries.reshape(N_DP, DEC_SEQ, full_width), out_grad.reshape(N_DP, DEC_SEQ, full_width), key_all.reshape(N_DP, ENC_SEQ, full_width), value_all.reshape(N_DP, ENC_SEQ, full_width), dec_segments.reshape(N_DP, DEC_SEQ), enc_segments.reshape(N_DP, ENC_SEQ))

    def one_pack(packed):
        return pack_grads(packed[0], packed[1], packed[2], packed[3], packed[4], packed[5])

    query_grad, key_grad, value_grad = lax.map(one_pack, stacked)
    query_grad = query_grad.reshape(DEC, full_width)
    key_round = key_grad.reshape(ENC, full_width).astype(jnp.bfloat16)
    value_round = value_grad.reshape(ENC, full_width).astype(jnp.bfloat16)
    enc_grad = (jnp.dot(key_round, w_key.T, preferred_element_type=jnp.float32) + jnp.dot(value_round, w_value.T, preferred_element_type=jnp.float32)).astype(jnp.bfloat16)
    w_key_grad = jnp.dot(enc_states.T, key_round, preferred_element_type=jnp.float32)
    w_value_grad = jnp.dot(enc_states.T, value_round, preferred_element_type=jnp.float32)
    return query_grad, enc_grad, w_key_grad, w_value_grad
```

```python
import functools

import jax
import jax.numpy as jnp
from jax import lax
from jax.experimental import pallas as pl
from jax.experimental.pallas import tpu as pltpu
from jax.sharding import PartitionSpec as P

HEAD_DIM = 128
NY, NZ, NC = 4, 4, 2
NX, NL = 4, 2
PEERS = NY * NC
ROWS = 128
KEYS = 384
ENC_ROWS = 12
FEATURES = 256
SHARED_Z = [[(y * NZ + z) * NC + c for y in range(NY) for c in range(NC)] for z in range(NZ)]
GROUPS = ((1, 3), (2, 0))
BF16, F32 = jnp.bfloat16, jnp.float32


def place():
    me = lax.axis_index("ctx")
    return me // (NZ * NC), (me // NC) % NZ, me % NC


def shift(value, dy=0, dz=0, dc=0):
    pairs = [
        ((y * NZ + z) * NC + c, (((y + dy) % NY) * NZ + (z + dz) % NZ) * NC + (c + dc) % NC)
        for y in range(NY)
        for z in range(NZ)
        for c in range(NC)
    ]
    return lax.ppermute(value, "ctx", pairs)


def by_owner(mine, arrived, me):
    blocks = [mine, *arrived]
    n = len(blocks)
    return jnp.stack([lax.select_n((owner - me) % n, *blocks) for owner in range(n)])


def gather_encoder(block):
    y, z, c = place()
    along_z = by_owner(block, [shift(block, dz=-d) for d in range(1, NZ)], z)
    along_y = by_owner(along_z, [shift(along_z, dy=-d) for d in range(1, NY)], y)
    other = shift(along_y, dc=1)
    first = c == 0
    both = jnp.stack([jnp.where(first, along_y, other), jnp.where(first, other, along_y)], axis=2)
    return both.reshape(NY * NZ * NC, *block.shape)


def sum_encoder(part):
    y, z, c = place()

    def at(value, index, axis):
        return lax.dynamic_index_in_dim(value, index, axis, keepdims=False)

    arrived = shift(at(part, 1 - c, 2), dc=1)
    total = (at(part, c, 2).astype(F32) + arrived.astype(F32)).astype(BF16)
    arrived = [shift(at(total, (y + d) % NY, 0), dy=d) for d in range(1, NY)]
    total = sum((a.astype(F32) for a in arrived), at(total, y, 0).astype(F32)).astype(BF16)
    arrived = [shift(at(total, (z + d) % NZ, 0), dz=d) for d in range(1, NZ)]
    return sum((a.astype(F32) for a in arrived), at(total, z, 0).astype(F32)).astype(BF16)


def columns_of(owner_y, distance, owner_c):
    z = lax.rem(lax.div(lax.axis_index("ctx"), NC), NZ)
    block = (owner_y * NZ + lax.rem(z + distance, NZ)) * NC + owner_c
    return pl.ds(pl.multiple_of(block * FEATURES, FEATURES), FEATURES)


def pack_kernel(group, queries, grads, out, sems):
    copies = []
    for peer in range(PEERS):
        for which, source in enumerate((queries, grads)):
            for i, distance in enumerate(group):
                copies.append(
                    pltpu.make_async_copy(
                        source.at[:, columns_of(peer // NC, distance, peer % NC)],
                        out.at[peer, which, :, pl.ds(i * FEATURES, FEATURES)],
                        sems.at[len(copies)],
                    )
                )
    for copy in copies:
        copy.start()
    for copy in copies:
        copy.wait()


def pack(group, queries, grads):
    shape = (PEERS, 2, ROWS, len(group) * FEATURES)
    return pl.pallas_call(
        functools.partial(pack_kernel, group),
        out_shape=jax.ShapeDtypeStruct(shape, BF16),
        in_specs=[pl.BlockSpec(memory_space=pl.ANY)] * 2,
        out_specs=pl.BlockSpec(memory_space=pl.ANY),
        scratch_shapes=[pltpu.SemaphoreType.DMA((PEERS * 2 * len(group),))],
        cost_estimate=pl.CostEstimate(flops=0, bytes_accessed=4 * PEERS * 2 * ROWS * len(group) * FEATURES, transcendentals=0),
    )(queries, grads)


def unpack_kernel(*refs):
    arrived, out, sems = refs[:-2], refs[-2], refs[-1]
    copies = []
    for group, source in zip(GROUPS, arrived, strict=True):
        for peer in range(PEERS):
            for i, distance in enumerate(group):
                copies.append(
                    pltpu.make_async_copy(
                        source.at[peer, :, pl.ds(i * FEATURES, FEATURES)],
                        out.at[:, columns_of(peer // NC, distance, peer % NC)],
                        sems.at[len(copies)],
                    )
                )
    for copy in copies:
        copy.start()
    for copy in copies:
        copy.wait()


def unpack(arrived):
    width = PEERS * NZ * FEATURES
    return pl.pallas_call(
        unpack_kernel,
        out_shape=jax.ShapeDtypeStruct((ROWS, width), BF16),
        in_specs=[pl.BlockSpec(memory_space=pl.ANY)] * len(arrived),
        out_specs=pl.BlockSpec(memory_space=pl.ANY),
        scratch_shapes=[pltpu.SemaphoreType.DMA((PEERS * NZ,))],
        cost_estimate=pl.CostEstimate(flops=0, bytes_accessed=4 * ROWS * width, transcendentals=0),
    )(*arrived)


def attend_kernel(ends, rows, key, value, query_grad, key_grad, value_grad, bias):
    tile = NC * ROWS

    @pl.when(pl.program_id(0) == 0)
    def _():
        z = lax.rem(lax.div(lax.axis_index("ctx"), NC), NZ)
        keys_at = lax.broadcasted_iota(jnp.int32, (KEYS, tile), 0)
        for y in range(NY):
            token = (y * NZ + z) * tile + lax.broadcasted_iota(jnp.int32, (1, tile), 1)
            low = jnp.zeros((1, tile), jnp.int32)
            high = jnp.full((1, tile), ends[0], jnp.int32)
            for d in range(3):
                past = token >= ends[3 + d]
                low = jnp.where(past, ends[d], low)
                high = jnp.where(past, ends[d + 1] if d < 2 else KEYS, high)
            allowed = (keys_at >= low) & (keys_at < high)
            bias[:, pl.ds(y * tile, tile)] = jnp.where(allowed, 0.0, -jnp.inf)

    keys, values = key[0], value[0]
    keys_turned = keys.T
    key_total = jnp.zeros((KEYS, HEAD_DIM), F32)
    value_total = jnp.zeros((KEYS, HEAD_DIM), F32)
    last = (((1,), (1,)), ((), ()))
    for y in range(NY):
        query = rows[pl.ds(y * NC, NC), 0].reshape(tile, HEAD_DIM)
        grad = rows[pl.ds(y * NC, NC), 1].reshape(tile, HEAD_DIM)
        scores = lax.dot_general(keys, query, last, preferred_element_type=F32)
        scores = scores + bias[:, pl.ds(y * tile, tile)]
        weights = jnp.exp(scores - jnp.max(scores, axis=0, keepdims=True))
        probability = weights * (1.0 / jnp.sum(weights, axis=0, keepdims=True))
        upstream = lax.dot_general(values, grad, last, preferred_element_type=F32)
        row_dot = jnp.sum(probability * upstream, axis=0, keepdims=True)
        score_grad = (probability * (upstream - row_dot)).astype(BF16)
        rounded = probability.astype(BF16)
        key_total += jnp.dot(score_grad, query, preferred_element_type=F32)
        value_total += jnp.dot(rounded, grad, preferred_element_type=F32)
        turned = jnp.dot(keys_turned, score_grad, preferred_element_type=F32)
        query_grad[pl.ds(y * NC, NC)] = turned.T.astype(BF16).reshape(NC, ROWS, HEAD_DIM)
    key_grad[0] = key_total.astype(BF16)
    value_grad[0] = value_total.astype(BF16)


def attend(ends, rows, key_values):
    count = key_values.shape[0]
    heads = FEATURES // HEAD_DIM
    elements = count * heads * PEERS * ROWS * KEYS
    block = (1, KEYS, HEAD_DIM)
    in_block = lambda h, ends: (h // heads, 0, h % heads)
    grads = jax.ShapeDtypeStruct((count, KEYS, FEATURES), BF16)
    return pl.pallas_call(
        attend_kernel,
        out_shape=(jax.ShapeDtypeStruct((PEERS, ROWS, count * FEATURES), BF16), grads, grads),
        grid_spec=pltpu.PrefetchScalarGridSpec(
            num_scalar_prefetch=1,
            grid=(count * heads,),
            in_specs=[
                pl.BlockSpec((PEERS, 2, ROWS, HEAD_DIM), lambda h, ends: (0, 0, 0, h)),
                pl.BlockSpec(block, in_block),
                pl.BlockSpec(block, lambda h, ends: (h // heads, 0, heads + h % heads)),
            ],
            out_specs=(
                pl.BlockSpec((PEERS, ROWS, HEAD_DIM), lambda h, ends: (0, 0, h)),
                pl.BlockSpec(block, in_block),
                pl.BlockSpec(block, in_block),
            ),
            scratch_shapes=[pltpu.VMEM((KEYS, PEERS * ROWS), F32)],
        ),
        compiler_params=pltpu.CompilerParams(vmem_limit_bytes=24 * 2**20),
        cost_estimate=pl.CostEstimate(
            flops=elements * HEAD_DIM * 10, bytes_accessed=6 * 2**20, transcendentals=elements
        ),
    )(ends, rows, key_values, key_values)


def body(queries, out_grad, enc_states, w_key, w_value, dec_segments, enc_segments):
    below = [jnp.sum(ids < d) for ids in (enc_segments, dec_segments) for d in range(1, 4)]
    counts = jnp.stack(below).astype(BF16)
    last_rows = jnp.pad(counts[None], ((0, 3), (0, enc_states.shape[1] - 6)))
    gathered = gather_encoder(jnp.concatenate([enc_states, last_rows], axis=0))
    encoder = gathered[:, :ENC_ROWS].reshape(KEYS, -1)
    ends = jnp.sum(gathered[:, ENC_ROWS, :6].astype(jnp.int32), axis=0)

    own_weight = jnp.concatenate([w_key, w_value], axis=1)
    copies = jnp.broadcast_to(own_weight[None], (NX * NL, *own_weight.shape))
    weight = lax.all_to_all(copies, "dp", 0, 0, tiled=True).reshape(-1, 2 * FEATURES)

    swap = functools.partial(
        lax.all_to_all,
        axis_name="ctx",
        split_axis=0,
        concat_axis=0,
        axis_index_groups=SHARED_Z,
        tiled=True,
    )
    rows = [swap(pack(group, queries, out_grad)) for group in GROUPS]

    own = jnp.dot(encoder, weight, preferred_element_type=F32).astype(BF16)
    key_values = {d: shift(own, dz=-d) if d else own for group in GROUPS for d in group}

    total, returned = 0.0, []
    for group, arrived in zip(GROUPS, rows, strict=True):
        query_grad, key_grad, value_grad = attend(
            ends, arrived, jnp.stack([key_values[d] for d in group])
        )
        returned.append(swap(query_grad))
        for i, d in enumerate(group):
            term = jnp.concatenate([key_grad[i], value_grad[i]], axis=1)
            total = total + (shift(term, dz=d) if d else term).astype(F32)
    query_grad = unpack(returned)

    rounded = total.astype(BF16)
    part = lax.dot_general(rounded, weight, (((1,), (1,)), ((), ())), preferred_element_type=F32)
    enc_grad = sum_encoder(part.astype(BF16).reshape(NY, NZ, NC, ENC_ROWS, -1))

    term = lax.dot_general(encoder, rounded, (((0,), (0,)), ((), ())), preferred_element_type=F32)
    pieces = term.astype(BF16).reshape(NX * NL, -1, 2 * FEATURES)
    pieces = lax.all_to_all(pieces, "dp", 0, 0, tiled=True)
    weight_grad = pieces.astype(F32).sum(axis=0)
    return query_grad, enc_grad, weight_grad[:, :FEATURES], weight_grad[:, FEATURES:]


def solution(mesh):
    tokens, weights, ids = P(("dp", "ctx"), None), P("dp", "ctx"), P(("dp", "ctx"))
    return jax.shard_map(
        body,
        mesh=mesh,
        in_specs=(tokens, tokens, tokens, weights, weights, ids, ids),
        out_specs=(tokens, tokens, weights, weights),
        check_vma=False,
    )
```

```python
import functools
import math

import jax
import jax.numpy as jnp
from jax import lax
from jax.experimental import pallas as pl
from jax.experimental.pallas import tpu as pltpu
from jax.sharding import PartitionSpec as P

HEAD_DIM = 128
NY, NZ, NC = 4, 4, 2
NX, NL = 4, 2
PEERS = NY * NC
ROWS = 128
KEYS = 384
ENC_ROWS = 12
FEATURES = 256
SHARED_Z = [[(y * NZ + z) * NC + c for y in range(NY) for c in range(NC)] for z in range(NZ)]
GROUPS = ((0, 2), (1, 3))
RETURNS = ((0,), (2,), (1, 3))
BF16, F32 = jnp.bfloat16, jnp.float32


def place():
    me = lax.axis_index("ctx")
    return me >> 3, (me >> 1) & 3, me & 1


def shift(value, dy=0, dz=0, dc=0):
    pairs = [
        ((y * NZ + z) * NC + c, (((y + dy) % NY) * NZ + (z + dz) % NZ) * NC + (c + dc) % NC)
        for y in range(NY)
        for z in range(NZ)
        for c in range(NC)
    ]
    return lax.ppermute(value, "ctx", pairs)


def by_owner(mine, arrived, me):
    blocks = [mine, *arrived]
    n = len(blocks)
    if n == 2:
        first = me == 0
        return jnp.stack([jnp.where(first, *blocks), jnp.where(first, *blocks[::-1])])
    return jnp.stack([lax.select_n((owner - me) & (n - 1), *blocks) for owner in range(n)])


def gather_encoder(block):
    y, z, c = place()
    along_z = by_owner(block, [shift(block, dz=-d) for d in range(1, NZ)], z)
    along_y = by_owner(along_z, [shift(along_z, dy=-d) for d in range(1, NY)], y)
    other = shift(along_y, dc=1)
    first = c == 0
    both = jnp.stack([jnp.where(first, along_y, other), jnp.where(first, other, along_y)], axis=2)
    return both.reshape(NY * NZ * NC, *block.shape)


def sum_encoder(part):
    y, z, c = place()

    def at(value, index, axis):
        start = [0] * value.ndim
        start[axis] = index
        size = [1 if i == axis else n for i, n in enumerate(value.shape)]
        return lax.dynamic_slice(value, start, size, allow_negative_indices=False).squeeze(axis)

    arrived = shift(at(part, 1 - c, 2), dc=1)
    total = (at(part, c, 2).astype(F32) + arrived.astype(F32)).astype(BF16)
    arrived = [shift(at(total, (y + d) & 3, 0), dy=d) for d in range(1, NY)]
    total = sum((a.astype(F32) for a in arrived), at(total, y, 0).astype(F32)).astype(BF16)
    arrived = [shift(at(total, (z + d) & 3, 0), dz=d) for d in range(1, NZ)]
    return sum((a.astype(F32) for a in arrived), at(total, z, 0).astype(F32)).astype(BF16)


def column_block(peer, distance, z):
    owner_y, owner_c = lax.div(peer, NC), lax.rem(peer, NC)
    return (owner_y * NZ + lax.rem(z + distance, NZ)) * NC + owner_c


def pack_kernel(z, *refs):
    sources, out = refs[:-1], refs[-1]
    for i in range(len(sources) // 2):
        for which in range(2):
            out[0, which, :, pl.ds(i * FEATURES, FEATURES)] = sources[2 * i + which][...]


def pack(group, z, queries, grads):
    shape = (2, ROWS, len(group) * FEATURES)
    columns = [
        pl.BlockSpec((ROWS, FEATURES), lambda p, z, d=d: (0, column_block(p, d, z[0])))
        for d in group
        for _ in range(2)
    ]
    return pl.pallas_call(
        pack_kernel,
        out_shape=jax.ShapeDtypeStruct((PEERS, *shape), BF16),
        grid_spec=pltpu.PrefetchScalarGridSpec(
            num_scalar_prefetch=1,
            grid=(PEERS,),
            in_specs=columns,
            out_specs=pl.BlockSpec((1, *shape), lambda p, z: (p, 0, 0, 0)),
        ),
        cost_estimate=pl.CostEstimate(
            flops=0, bytes_accessed=4 * PEERS * math.prod(shape), transcendentals=0
        ),
    )(z, *[queries, grads] * len(group))


def unpack_kernel(z, *refs):
    sources, out = refs[:-1], refs[-1]
    for group, source in zip(RETURNS, sources, strict=True):
        for i, distance in enumerate(group):
            for c in range(NC):
                at = (lax.rem(z[0] + distance, NZ) * NC + c) * FEATURES
                columns = pl.ds(pl.multiple_of(at, FEATURES), FEATURES)
                out[:, columns] = source[c, :, pl.ds(i * FEATURES, FEATURES)]


def unpack(z, arrived):
    width = NZ * NC * FEATURES
    return pl.pallas_call(
        unpack_kernel,
        out_shape=jax.ShapeDtypeStruct((ROWS, NY * width), BF16),
        grid_spec=pltpu.PrefetchScalarGridSpec(
            num_scalar_prefetch=1,
            grid=(NY,),
            in_specs=[
                pl.BlockSpec((NC, ROWS, a.shape[2]), lambda y, z: (y, 0, 0)) for a in arrived
            ],
            out_specs=pl.BlockSpec((ROWS, width), lambda y, z: (0, y)),
        ),
        cost_estimate=pl.CostEstimate(
            flops=0, bytes_accessed=4 * ROWS * NY * width, transcendentals=0
        ),
    )(z, *arrived)


def attend_kernel(ends, rows, key, value, query_grad, key_grad, value_grad, bias):
    tile = NC * ROWS

    @pl.when(pl.program_id(0) == 0)
    def _():
        z = lax.rem(lax.div(lax.axis_index("ctx"), NC), NZ)
        keys_at = lax.broadcasted_iota(jnp.int32, (KEYS, tile), 0)
        for y in range(NY):
            token = (y * NZ + z) * tile + lax.broadcasted_iota(jnp.int32, (1, tile), 1)
            low = jnp.zeros((1, tile), jnp.int32)
            high = jnp.full((1, tile), ends[0], jnp.int32)
            for d in range(3):
                past = token >= ends[3 + d]
                low = jnp.where(past, ends[d], low)
                high = jnp.where(past, ends[d + 1] if d < 2 else KEYS, high)
            allowed = (keys_at >= low) & (keys_at < high)
            bias[:, pl.ds(y * tile, tile)] = jnp.where(allowed, 0.0, -jnp.inf)

    keys, values = key[0], value[0]
    keys_turned = keys.T
    key_total = jnp.zeros((KEYS, HEAD_DIM), F32)
    value_total = jnp.zeros((KEYS, HEAD_DIM), F32)
    last = (((1,), (1,)), ((), ()))
    for y in range(NY):
        query = rows[pl.ds(y * NC, NC), 0].reshape(tile, HEAD_DIM)
        grad = rows[pl.ds(y * NC, NC), 1].reshape(tile, HEAD_DIM)
        scores = lax.dot_general(keys, query, last, preferred_element_type=F32)
        scores = scores + bias[:, pl.ds(y * tile, tile)]
        weights = jnp.exp(scores - jnp.max(scores, axis=0, keepdims=True))
        probability = weights * (1.0 / jnp.sum(weights, axis=0, keepdims=True))
        upstream = lax.dot_general(values, grad, last, preferred_element_type=F32)
        row_dot = jnp.sum(probability * upstream, axis=0, keepdims=True)
        score_grad = (probability * (upstream - row_dot)).astype(BF16)
        rounded = probability.astype(BF16)
        key_total += jnp.dot(score_grad, query, preferred_element_type=F32)
        value_total += jnp.dot(rounded, grad, preferred_element_type=F32)
        turned = jnp.dot(keys_turned, score_grad, preferred_element_type=F32)
        query_grad[pl.ds(y * NC, NC)] = turned.T.astype(BF16).reshape(NC, ROWS, HEAD_DIM)
    key_grad[0] = key_total.astype(BF16)
    value_grad[0] = value_total.astype(BF16)


def attend(ends, rows, first, keys, values):
    count = keys.shape[0]
    heads = FEATURES // HEAD_DIM
    elements = count * heads * PEERS * ROWS * KEYS
    block = (1, KEYS, HEAD_DIM)
    in_block = lambda h, ends: (h // heads, 0, h % heads)
    grads = jax.ShapeDtypeStruct((count, KEYS, FEATURES), BF16)
    return pl.pallas_call(
        attend_kernel,
        out_shape=(jax.ShapeDtypeStruct((PEERS, ROWS, count * FEATURES), BF16), grads, grads),
        grid_spec=pltpu.PrefetchScalarGridSpec(
            num_scalar_prefetch=1,
            grid=(count * heads,),
            in_specs=[
                pl.BlockSpec(
                    (PEERS, 2, ROWS, HEAD_DIM), lambda h, ends: (0, 0, 0, first * heads + h)
                ),
                pl.BlockSpec(block, in_block),
                pl.BlockSpec(block, in_block),
            ],
            out_specs=(
                pl.BlockSpec((PEERS, ROWS, HEAD_DIM), lambda h, ends: (0, 0, h)),
                pl.BlockSpec(block, in_block),
                pl.BlockSpec(block, in_block),
            ),
            scratch_shapes=[pltpu.VMEM((KEYS, PEERS * ROWS), F32)],
        ),
        compiler_params=pltpu.CompilerParams(vmem_limit_bytes=24 * 2**20),
        cost_estimate=pl.CostEstimate(
            flops=elements * HEAD_DIM * 10, bytes_accessed=6 * 2**20, transcendentals=elements
        ),
    )(ends, rows, keys, values)


def gather_weights(block):
    me = lax.axis_index("dp")
    x, low = me >> 1, me & 1

    def ahead(value, dx, dl):
        pairs = [
            (a * NL + b, (a - dx) % NX * NL + (b - dl) % NL) for a in range(NX) for b in range(NL)
        ]
        return lax.ppermute(value, "dp", pairs)

    pair = by_owner(block, [ahead(block, 0, 1)], low)
    return by_owner(pair, [ahead(pair, d, 0) for d in range(1, NX)], x).reshape(-1, block.shape[1])


def body(queries, out_grad, enc_states, w_key, w_value, dec_segments, enc_segments):
    z = place()[1]
    z_index = z.reshape(1)
    below = [jnp.sum(ids < d) for ids in (enc_segments, dec_segments) for d in range(1, 4)]
    counts = jnp.stack(below).astype(BF16)
    last_rows = jnp.pad(counts[None], ((0, 3), (0, enc_states.shape[1] - 6)))
    gathered = gather_encoder(jnp.concatenate([enc_states, last_rows], axis=0))
    encoder = gathered[:, :ENC_ROWS].reshape(KEYS, -1)
    ends = jnp.sum(gathered[:, ENC_ROWS, :6].astype(jnp.int32), axis=0)
    weight = gather_weights(jnp.concatenate([w_key, w_value], axis=1))

    swap = functools.partial(
        lax.all_to_all,
        axis_name="ctx",
        split_axis=0,
        concat_axis=0,
        axis_index_groups=SHARED_Z,
        tiled=True,
    )
    near = swap(pack(GROUPS[0], z_index, queries, out_grad))
    own = jnp.dot(encoder, weight, preferred_element_type=F32).astype(BF16)
    far_packed, near = lax.optimization_barrier((pack(GROUPS[1], z_index, queries, out_grad), near))
    far = swap(far_packed)

    ahead, behind = shift(own, dz=-1), shift(own, dz=1)
    key_of = lambda block: block[:, :FEATURES]
    value_of = lambda block: block[:, FEATURES:]
    key_opposite, value_opposite = shift(key_of(ahead), dz=-1), shift(value_of(behind), dz=1)

    back_0, key_0, value_0 = attend(ends, near, 0, key_of(own)[None], value_of(own)[None])
    back_2, key_2, value_2 = attend(ends, near, 1, key_opposite[None], value_opposite[None])
    back_1, key_1, value_1 = attend(
        ends,
        far,
        0,
        jnp.stack([key_of(ahead), key_of(behind)]),
        jnp.stack([value_of(ahead), value_of(behind)]),
    )
    query_grad = unpack(z_index, [swap(back_0), swap(back_2), swap(back_1)])

    def joined(a, b):
        return (a.astype(F32) + b.astype(F32)).astype(BF16)

    key_ahead = joined(key_1[0], shift(key_2[0], dz=1))
    value_behind = joined(value_1[1], shift(value_2[0], dz=-1))
    total = jnp.concatenate([key_0[0], value_0[0]], axis=1).astype(F32)
    total += shift(jnp.concatenate([key_ahead, value_1[0]], axis=1), dz=1).astype(F32)
    total += shift(jnp.concatenate([key_1[1], value_behind], axis=1), dz=-1).astype(F32)

    rounded = total.astype(BF16)
    part = lax.dot_general(rounded, weight, (((1,), (1,)), ((), ())), preferred_element_type=F32)
    enc_grad = sum_encoder(part.astype(BF16).reshape(NY, NZ, NC, ENC_ROWS, -1))

    term = lax.dot_general(encoder, rounded, (((0,), (0,)), ((), ())), preferred_element_type=F32)
    pieces = term.astype(BF16).reshape(NX * NL, -1, 2 * FEATURES)
    pieces = lax.all_to_all(pieces, "dp", 0, 0, tiled=True)
    weight_grad = pieces.astype(F32).sum(axis=0)
    return query_grad, enc_grad, weight_grad[:, :FEATURES], weight_grad[:, FEATURES:]


def solution(mesh):
    tokens, weights, ids = P(("dp", "ctx"), None), P("dp", "ctx"), P(("dp", "ctx"))
    return jax.shard_map(
        body,
        mesh=mesh,
        in_specs=(tokens, tokens, tokens, weights, weights, ids, ids),
        out_specs=(tokens, tokens, weights, weights),
        check_vma=False,
    )
```

```python
import functools
import math

import jax
import jax.numpy as jnp
from jax import lax
from jax.experimental import pallas as pl
from jax.experimental.pallas import tpu as pltpu
from jax.sharding import PartitionSpec as P

HEAD_DIM = 128
NY, NZ, NC = 4, 4, 2
NX, NL = 4, 2
PEERS = NY * NC
ROWS = 128
KEYS = 384
ENC_ROWS = 12
FEATURES = 256
SHARED_Z = [[(y * NZ + z) * NC + c for y in range(NY) for c in range(NC)] for z in range(NZ)]
GROUPS = ((0, 2), (1, 3))

BF16, F32 = jnp.bfloat16, jnp.float32


def place():
    me = lax.axis_index("ctx")
    return me >> 3, (me >> 1) & 3, me & 1


def shift(value, dy=0, dz=0, dc=0):
    pairs = [
        ((y * NZ + z) * NC + c, (((y + dy) % NY) * NZ + (z + dz) % NZ) * NC + (c + dc) % NC)
        for y in range(NY)
        for z in range(NZ)
        for c in range(NC)
    ]
    return lax.ppermute(value, "ctx", pairs)


def by_owner(mine, arrived, me):
    blocks = [mine, *arrived]
    n = len(blocks)
    if n == 2:
        first = me == 0
        return jnp.stack([jnp.where(first, *blocks), jnp.where(first, *blocks[::-1])])
    return jnp.stack([lax.select_n((owner - me) & (n - 1), *blocks) for owner in range(n)])


def gather_encoder(block, later):
    y, z, c = place()
    along_y = by_owner(block, [shift(block, dy=-d) for d in range(1, NY)], y)
    along_y, later = lax.optimization_barrier((along_y, later))
    along_z = by_owner(along_y, [shift(along_y, dz=-d) for d in range(1, NZ)], z)
    other = shift(along_z, dc=1)
    first = c == 0
    both = [jnp.where(first, along_z, other), jnp.where(first, other, along_z)]
    gathered = jnp.stack(both, axis=2).swapaxes(0, 1)
    return gathered.reshape(NY * NZ * NC, *block.shape), later


def sum_encoder(part, later):
    y, z, c = place()

    def at(value, index, axis):
        start = [0] * value.ndim
        start[axis] = index
        size = [1 if i == axis else n for i, n in enumerate(value.shape)]
        return lax.dynamic_slice(value, start, size, allow_negative_indices=False).squeeze(axis)

    sent, later = lax.optimization_barrier((at(part, 1 - c, 2), later))
    arrived = shift(sent, dc=1)
    total = (at(part, c, 2).astype(F32) + arrived.astype(F32)).astype(BF16)
    arrived = [shift(at(total, (y + d) & 3, 0), dy=d) for d in range(1, NY)]
    total = sum((a.astype(F32) for a in arrived), at(total, y, 0).astype(F32)).astype(BF16)
    arrived = [shift(at(total, (z + d) & 3, 0), dz=d) for d in range(1, NZ)]
    return sum((a.astype(F32) for a in arrived), at(total, z, 0).astype(F32)).astype(BF16), later


def pack_kernel(z, *refs):
    sources, out = refs[:-1], refs[-1]
    for i in range(len(sources) // 2):
        for which in range(2):
            for c in range(NC):
                block = sources[2 * i + which][:, pl.ds(c * FEATURES, FEATURES)]
                out[c, which, :, pl.ds(i * FEATURES, FEATURES)] = block


def pack(group, z, queries, grads):
    shape = (2, ROWS, len(group) * FEATURES)
    columns = [
        pl.BlockSpec((ROWS, NC * FEATURES), lambda y, z, d=d: (0, y * NZ + lax.rem(z[0] + d, NZ)))
        for d in group
        for _ in range(2)
    ]
    return pl.pallas_call(
        pack_kernel,
        out_shape=jax.ShapeDtypeStruct((PEERS, *shape), BF16),
        grid_spec=pltpu.PrefetchScalarGridSpec(
            num_scalar_prefetch=1,
            grid=(NY,),
            in_specs=columns,
            out_specs=pl.BlockSpec((NC, *shape), lambda y, z: (y, 0, 0, 0)),
        ),
        cost_estimate=pl.CostEstimate(
            flops=0, bytes_accessed=4 * PEERS * math.prod(shape), transcendentals=0
        ),
    )(z, *[queries, grads] * len(group))


def unpack_kernel(z, *refs):
    sources, out = refs[:-1], refs[-1]
    for group, source in zip(GROUPS, sources, strict=True):
        for i, distance in enumerate(group):
            for c in range(NC):
                at = (lax.rem(z[0] + distance, NZ) * NC + c) * FEATURES
                columns = pl.ds(pl.multiple_of(at, FEATURES), FEATURES)
                out[:, columns] = source[c, :, pl.ds(i * FEATURES, FEATURES)]


def unpack(z, arrived):
    width = NZ * NC * FEATURES
    return pl.pallas_call(
        unpack_kernel,
        out_shape=jax.ShapeDtypeStruct((ROWS, NY * width), BF16),
        grid_spec=pltpu.PrefetchScalarGridSpec(
            num_scalar_prefetch=1,
            grid=(NY,),
            in_specs=[
                pl.BlockSpec((NC, ROWS, a.shape[2]), lambda y, z: (y, 0, 0)) for a in arrived
            ],
            out_specs=pl.BlockSpec((ROWS, width), lambda y, z: (0, y)),
        ),
        cost_estimate=pl.CostEstimate(
            flops=0, bytes_accessed=4 * ROWS * NY * width, transcendentals=0
        ),
    )(z, *arrived)


def attend_kernel(ends, rows, key, value, *refs):
    query_grad, key_grad, value_grad, bias = refs[-4:]
    tile = NC * ROWS

    @pl.when(pl.program_id(0) == 0)
    def _():
        z = lax.rem(lax.div(lax.axis_index("ctx"), NC), NZ)
        keys_at = lax.broadcasted_iota(jnp.int32, (KEYS, tile), 0)
        for y in range(NY):
            token = (y * NZ + z) * tile + lax.broadcasted_iota(jnp.int32, (1, tile), 1)
            low = jnp.zeros((1, tile), jnp.int32)
            high = jnp.full((1, tile), ends[0], jnp.int32)
            for d in range(3):
                past = token >= ends[3 + d]
                low = jnp.where(past, ends[d], low)
                high = jnp.where(past, ends[d + 1] if d < 2 else KEYS, high)
            allowed = (keys_at >= low) & (keys_at < high)
            bias[:, pl.ds(y * tile, tile)] = jnp.where(allowed, 0.0, -jnp.inf)

    keys, values = key[0], value[0]
    keys_turned = keys.T
    key_total = jnp.zeros((KEYS, HEAD_DIM), F32)
    value_total = jnp.zeros((KEYS, HEAD_DIM), F32)
    last = (((1,), (1,)), ((), ()))
    for y in range(NY):
        query = rows[pl.ds(y * NC, NC), 0].reshape(tile, HEAD_DIM)
        grad = rows[pl.ds(y * NC, NC), 1].reshape(tile, HEAD_DIM)
        scores = lax.dot_general(keys, query, last, preferred_element_type=F32)
        scores = scores + bias[:, pl.ds(y * tile, tile)]
        weights = jnp.exp(scores - jnp.max(scores, axis=0, keepdims=True))
        probability = weights * (1.0 / jnp.sum(weights, axis=0, keepdims=True))
        upstream = lax.dot_general(values, grad, last, preferred_element_type=F32)
        row_dot = jnp.sum(probability * upstream, axis=0, keepdims=True)
        score_grad = (probability * (upstream - row_dot)).astype(BF16)
        rounded = probability.astype(BF16)
        key_total += jnp.dot(score_grad, query, preferred_element_type=F32)
        value_total += jnp.dot(rounded, grad, preferred_element_type=F32)
        turned = jnp.dot(keys_turned, score_grad, preferred_element_type=F32)
        query_grad[pl.ds(y * NC, NC)] = turned.T.astype(BF16).reshape(NC, ROWS, HEAD_DIM)
    key_grad[0] = key_total.astype(BF16)
    value_grad[0] = value_total.astype(BF16)


def attend(ends, rows, first, keys, values, into=None):
    count = keys.shape[0]
    heads = FEATURES // HEAD_DIM
    given = [] if into is None else [into]
    elements = count * heads * PEERS * ROWS * KEYS
    block = (1, KEYS, HEAD_DIM)
    in_block = lambda h, ends: (h // heads, 0, h % heads)
    grads = jax.ShapeDtypeStruct((count, KEYS, FEATURES), BF16)
    return pl.pallas_call(
        attend_kernel,
        out_shape=(jax.ShapeDtypeStruct((PEERS, ROWS, rows.shape[3]), BF16), grads, grads),
        grid_spec=pltpu.PrefetchScalarGridSpec(
            num_scalar_prefetch=1,
            grid=(count * heads,),
            in_specs=[
                pl.BlockSpec(
                    (PEERS, 2, ROWS, HEAD_DIM), lambda h, ends: (0, 0, 0, first * heads + h)
                ),
                pl.BlockSpec(block, in_block),
                pl.BlockSpec(block, in_block),
                *[pl.BlockSpec(memory_space=pl.ANY) for _ in given],
            ],
            out_specs=(
                pl.BlockSpec((PEERS, ROWS, HEAD_DIM), lambda h, ends: (0, 0, first * heads + h)),
                pl.BlockSpec(block, in_block),
                pl.BlockSpec(block, in_block),
            ),
            scratch_shapes=[pltpu.VMEM((KEYS, PEERS * ROWS), F32)],
        ),
        compiler_params=pltpu.CompilerParams(vmem_limit_bytes=24 * 2**20),
        cost_estimate=pl.CostEstimate(
            flops=elements * HEAD_DIM * 10, bytes_accessed=6 * 2**20, transcendentals=elements
        ),
        input_output_aliases={4: 0} if given else {},
    )(ends, rows, keys, values, *given)


def gather_weights(block):
    me = lax.axis_index("dp")
    held = block[None]
    for bit in (1, 2, 4):
        other = lax.ppermute(held, "dp", [(d, d ^ bit) for d in range(NX * NL)])
        first = (me & bit) == 0
        held = jnp.concatenate([jnp.where(first, held, other), jnp.where(first, other, held)])
    return held.reshape(-1, block.shape[1])


def body(queries, out_grad, enc_states, w_key, w_value, dec_segments, enc_segments):
    z = place()[1]
    z_index = z.reshape(1)
    width = enc_states.shape[1]
    ids = [jnp.pad(i.astype(BF16)[None], ((0, 0), (0, width - i.size))) for i in (enc_segments, dec_segments)]
    block = jnp.concatenate([enc_states, *ids, jnp.zeros((2, width), BF16)], axis=0)
    gathered, z_later = gather_encoder(block, z_index)
    encoder = gathered[:, :ENC_ROWS].reshape(KEYS, -1)
    all_ids = (gathered[:, ENC_ROWS, :ENC_ROWS], gathered[:, ENC_ROWS + 1, :ROWS])
    first_of = jnp.arange(1, 4, dtype=BF16)[:, None, None]
    ends = jnp.concatenate([jnp.sum((i[None] < first_of).astype(jnp.int32), axis=(1, 2)) for i in all_ids])
    weight = gather_weights(jnp.concatenate([w_key, w_value], axis=1))

    swap = functools.partial(
        lax.all_to_all,
        axis_name="ctx",
        split_axis=0,
        concat_axis=0,
        axis_index_groups=SHARED_Z,
        tiled=True,
    )
    near = swap(pack(GROUPS[0], z_index, queries, out_grad))
    own = jnp.dot(encoder, weight, preferred_element_type=F32).astype(BF16)
    far_packed, near = lax.optimization_barrier((pack(GROUPS[1], z_later, queries, out_grad), near))
    far = swap(far_packed)

    ahead, behind = shift(own, dz=-1), shift(own, dz=1)
    key_of = lambda block: block[:, :FEATURES]
    value_of = lambda block: block[:, FEATURES:]
    key_opposite, value_opposite = shift(key_of(ahead), dz=-1), shift(value_of(behind), dz=1)

    back, key_0, value_0 = attend(ends, near, 0, key_of(own)[None], value_of(own)[None])
    back, key_2, value_2 = attend(ends, near, 1, key_opposite[None], value_opposite[None], back)
    back_near = swap(back)
    back, key_1, value_1 = attend(
        ends,
        far,
        0,
        jnp.stack([key_of(ahead), key_of(behind)]),
        jnp.stack([value_of(ahead), value_of(behind)]),
    )

    def joined(a, b):
        return (a.astype(F32) + b.astype(F32)).astype(BF16)

    key_ahead = joined(key_1[0], shift(key_2[0], dz=1))
    value_behind = joined(value_1[1], shift(value_2[0], dz=-1))
    for_ahead = jnp.concatenate([key_ahead, value_1[0]], axis=1)
    for_behind = jnp.concatenate([key_1[1], value_behind], axis=1)
    for_ahead, for_behind, back = lax.optimization_barrier((for_ahead, for_behind, back))
    total = jnp.concatenate([key_0[0], value_0[0]], axis=1).astype(F32)
    total += shift(for_ahead, dz=1).astype(F32) + shift(for_behind, dz=-1).astype(F32)

    query_grad = unpack(z_index, [back_near, swap(back)])
    total, query_grad = lax.optimization_barrier((total, query_grad))

    rounded = total.astype(BF16)
    part = lax.dot_general(rounded, weight, (((1,), (1,)), ((), ())), preferred_element_type=F32)
    part = part.astype(BF16).reshape(NY, NZ, NC, ENC_ROWS, -1)
    enc_grad, encoder = sum_encoder(part, encoder)

    term = lax.dot_general(encoder, rounded, (((0,), (0,)), ((), ())), preferred_element_type=F32)
    pieces = term.astype(BF16).reshape(NX * NL, -1, 2 * FEATURES)
    pieces = lax.all_to_all(pieces, "dp", 0, 0, tiled=True)
    weight_grad = pieces.astype(F32).sum(axis=0)
    return query_grad, enc_grad, weight_grad[:, :FEATURES], weight_grad[:, FEATURES:]


def solution(mesh):
    tokens, weights, ids = P(("dp", "ctx"), None), P("dp", "ctx"), P(("dp", "ctx"))
    return jax.shard_map(
        body,
        mesh=mesh,
        in_specs=(tokens, tokens, tokens, weights, weights, ids, ids),
        out_specs=(tokens, tokens, weights, weights),
        check_vma=False,
    )
```

```python
import functools
import math

import jax
import jax.numpy as jnp
from jax import lax
from jax.experimental import pallas as pl
from jax.experimental.pallas import tpu as pltpu
from jax.sharding import PartitionSpec as P

HEAD_DIM = 128
NY, NZ, NC = 4, 4, 2
NX, NL = 4, 2
PEERS = NY * NC
ROWS = 128
KEYS = 384
ENC_ROWS = 12
FEATURES = 256
SHARED_Z = [[(y * NZ + z) * NC + c for y in range(NY) for c in range(NC)] for z in range(NZ)]
GROUPS = ((0, 2), (1, 3))

BF16, F32 = jnp.bfloat16, jnp.float32


def place():
    me = lax.axis_index("ctx")
    return me >> 3, (me >> 1) & 3, me & 1


def shift(value, dy=0, dz=0, dc=0):
    pairs = [
        ((y * NZ + z) * NC + c, (((y + dy) % NY) * NZ + (z + dz) % NZ) * NC + (c + dc) % NC)
        for y in range(NY)
        for z in range(NZ)
        for c in range(NC)
    ]
    return lax.ppermute(value, "ctx", pairs)


def by_owner(mine, arrived, me):
    blocks = [mine, *arrived]
    n = len(blocks)
    if n == 2:
        first = me == 0
        return jnp.stack([jnp.where(first, *blocks), jnp.where(first, *blocks[::-1])])
    return jnp.stack([lax.select_n((owner - me) & (n - 1), *blocks) for owner in range(n)])


def double(held, bit):
    other = lax.ppermute(held, "dp", [(d, d ^ bit) for d in range(NX * NL)])
    first = (lax.axis_index("dp") & bit) == 0
    return jnp.concatenate([jnp.where(first, held, other), jnp.where(first, other, held)])


def along_x(pair):
    x = lax.axis_index("dp") >> 1

    def from_ahead(d):
        pairs = [(a * NL + b, (a - d) % NX * NL + b) for a in range(NX) for b in range(NL)]
        return lax.ppermute(pair, "dp", pairs)

    return by_owner(pair, [from_ahead(d) for d in range(1, NX)], x).reshape(-1, *pair.shape[1:])


def gather(block, weight, packed, later):
    y, z, c = place()
    weight = double(weight[None], 1)
    along_y = by_owner(block, [shift(block, dy=-d) for d in range(1, NY)], y)
    along_y, weight, packed = lax.optimization_barrier((along_y, weight, packed))
    weight = along_x(weight)
    along_z = by_owner(along_y, [shift(along_y, dz=-d) for d in range(1, NZ)], z)
    along_z, later = lax.optimization_barrier((along_z, later))
    other = shift(along_z, dc=1)
    first = c == 0
    both = [jnp.where(first, along_z, other), jnp.where(first, other, along_z)]
    gathered = jnp.stack(both, axis=2).swapaxes(0, 1)
    return gathered.reshape(NY * NZ * NC, *block.shape), weight.reshape(-1, weight.shape[2]), packed, later


def sum_encoder(part, later, last):
    y, z, c = place()

    def at(value, index, axis):
        start = [0] * value.ndim
        start[axis] = index
        size = [1 if i == axis else n for i, n in enumerate(value.shape)]
        return lax.dynamic_slice(value, start, size, allow_negative_indices=False).squeeze(axis)

    sent, later = lax.optimization_barrier((at(part, 1 - c, 2), later))
    arrived = shift(sent, dc=1)
    total = (at(part, c, 2).astype(F32) + arrived.astype(F32)).astype(BF16)
    arrived = [shift(at(total, (y + d) & 3, 0), dy=d) for d in range(1, NY)]
    total = sum((a.astype(F32) for a in arrived), at(total, y, 0).astype(F32)).astype(BF16)
    total, last = lax.optimization_barrier((total, last))
    arrived = [shift(at(total, (z + d) & 3, 0), dz=d) for d in range(1, NZ)]
    return sum((a.astype(F32) for a in arrived), at(total, z, 0).astype(F32)).astype(BF16), later, last


def pack_kernel(z, *refs):
    sources, out = refs[:-1], refs[-1]
    for i in range(len(sources) // 2):
        for which in range(2):
            for c in range(NC):
                block = sources[2 * i + which][:, pl.ds(c * FEATURES, FEATURES)]
                out[c, which, :, pl.ds(i * FEATURES, FEATURES)] = block


def pack(group, z, queries, grads):
    shape = (2, ROWS, len(group) * FEATURES)
    columns = [
        pl.BlockSpec((ROWS, NC * FEATURES), lambda y, z, d=d: (0, y * NZ + lax.rem(z[0] + d, NZ)))
        for d in group
        for _ in range(2)
    ]
    return pl.pallas_call(
        pack_kernel,
        out_shape=jax.ShapeDtypeStruct((PEERS, *shape), BF16),
        grid_spec=pltpu.PrefetchScalarGridSpec(
            num_scalar_prefetch=1,
            grid=(NY,),
            in_specs=columns,
            out_specs=pl.BlockSpec((NC, *shape), lambda y, z: (y, 0, 0, 0)),
        ),
        cost_estimate=pl.CostEstimate(
            flops=0, bytes_accessed=4 * PEERS * math.prod(shape), transcendentals=0
        ),
    )(z, *[queries, grads] * len(group))


def unpack_kernel(z, source, *refs):
    out = refs[-1]
    for c in range(NC):
        out[:, pl.ds(c * FEATURES, FEATURES)] = source[c]


def unpack(group, z, arrived, into=None):
    assert group[1] == group[0] + 2
    width = NC * FEATURES
    given = [] if into is None else [into]
    return pl.pallas_call(
        unpack_kernel,
        out_shape=jax.ShapeDtypeStruct((ROWS, NY * NZ * width), BF16),
        grid_spec=pltpu.PrefetchScalarGridSpec(
            num_scalar_prefetch=1,
            grid=(NY, 2),
            in_specs=[
                pl.BlockSpec((NC, ROWS, FEATURES), lambda y, i, z: (y, 0, i)),
                *[pl.BlockSpec(memory_space=pl.ANY) for _ in given],
            ],
            out_specs=pl.BlockSpec(
                (ROWS, width), lambda y, i, z: (0, y * NZ + lax.rem(z[0] + group[0] + 2 * i, NZ))
            ),
        ),
        input_output_aliases={2: 0} if given else {},
        cost_estimate=pl.CostEstimate(
            flops=0, bytes_accessed=4 * ROWS * NY * 2 * width, transcendentals=0
        ),
    )(z, arrived, *given)


def attend_kernel(ends, rows, key, value, *refs):
    query_grad, key_grad, value_grad, bias = refs[-4:]
    tile = NC * ROWS

    @pl.when(pl.program_id(0) == 0)
    def _():
        z = lax.rem(lax.div(lax.axis_index("ctx"), NC), NZ)
        keys_at = lax.broadcasted_iota(jnp.int32, (KEYS, tile), 0)
        for y in range(NY):
            token = (y * NZ + z) * tile + lax.broadcasted_iota(jnp.int32, (1, tile), 1)
            low = jnp.zeros((1, tile), jnp.int32)
            high = jnp.full((1, tile), ends[0], jnp.int32)
            for d in range(3):
                past = token >= ends[3 + d]
                low = jnp.where(past, ends[d], low)
                high = jnp.where(past, ends[d + 1] if d < 2 else KEYS, high)
            allowed = (keys_at >= low) & (keys_at < high)
            bias[:, pl.ds(y * tile, tile)] = jnp.where(allowed, 0.0, -jnp.inf)

    keys, values = key[0], value[0]
    keys_turned = keys.T
    key_total = jnp.zeros((KEYS, HEAD_DIM), F32)
    value_total = jnp.zeros((KEYS, HEAD_DIM), F32)
    last = (((1,), (1,)), ((), ()))
    for y in range(NY):
        query = rows[pl.ds(y * NC, NC), 0].reshape(tile, HEAD_DIM)
        grad = rows[pl.ds(y * NC, NC), 1].reshape(tile, HEAD_DIM)
        scores = lax.dot_general(keys, query, last, preferred_element_type=F32)
        scores = scores + bias[:, pl.ds(y * tile, tile)]
        weights = jnp.exp(scores - jnp.max(scores, axis=0, keepdims=True))
        probability = weights * (1.0 / jnp.sum(weights, axis=0, keepdims=True))
        upstream = lax.dot_general(values, grad, last, preferred_element_type=F32)
        row_dot = jnp.sum(probability * upstream, axis=0, keepdims=True)
        score_grad = (probability * (upstream - row_dot)).astype(BF16)
        rounded = probability.astype(BF16)
        key_total += jnp.dot(score_grad, query, preferred_element_type=F32)
        value_total += jnp.dot(rounded, grad, preferred_element_type=F32)
        turned = jnp.dot(keys_turned, score_grad, preferred_element_type=F32)
        query_grad[pl.ds(y * NC, NC)] = turned.T.astype(BF16).reshape(NC, ROWS, HEAD_DIM)
    key_grad[0] = key_total.astype(BF16)
    value_grad[0] = value_total.astype(BF16)


def attend(ends, rows, first, keys, values, into=None):
    count = keys.shape[0]
    heads = FEATURES // HEAD_DIM
    given = [] if into is None else [into]
    elements = count * heads * PEERS * ROWS * KEYS
    block = (1, KEYS, HEAD_DIM)
    in_block = lambda h, ends: (h // heads, 0, h % heads)
    grads = jax.ShapeDtypeStruct((count, KEYS, FEATURES), BF16)
    return pl.pallas_call(
        attend_kernel,
        out_shape=(jax.ShapeDtypeStruct((PEERS, ROWS, rows.shape[3]), BF16), grads, grads),
        grid_spec=pltpu.PrefetchScalarGridSpec(
            num_scalar_prefetch=1,
            grid=(count * heads,),
            in_specs=[
                pl.BlockSpec(
                    (PEERS, 2, ROWS, HEAD_DIM), lambda h, ends: (0, 0, 0, first * heads + h)
                ),
                pl.BlockSpec(block, in_block),
                pl.BlockSpec(block, in_block),
                *[pl.BlockSpec(memory_space=pl.ANY) for _ in given],
            ],
            out_specs=(
                pl.BlockSpec((PEERS, ROWS, HEAD_DIM), lambda h, ends: (0, 0, first * heads + h)),
                pl.BlockSpec(block, in_block),
                pl.BlockSpec(block, in_block),
            ),
            scratch_shapes=[pltpu.VMEM((KEYS, PEERS * ROWS), F32)],
        ),
        compiler_params=pltpu.CompilerParams(vmem_limit_bytes=24 * 2**20),
        cost_estimate=pl.CostEstimate(
            flops=elements * HEAD_DIM * 10, bytes_accessed=6 * 2**20, transcendentals=elements
        ),
        input_output_aliases={4: 0} if given else {},
    )(ends, rows, keys, values, *given)


def body(queries, out_grad, enc_states, w_key, w_value, dec_segments, enc_segments):
    z = place()[1]
    z_index = z.reshape(1)
    width = enc_states.shape[1]
    ids = [jnp.pad(i.astype(BF16)[None], ((0, 0), (0, width - i.size))) for i in (enc_segments, dec_segments)]
    block = jnp.concatenate([enc_states, *ids, jnp.zeros((2, width), BF16)], axis=0)
    gathered, weight, near_packed, z_later = gather(
        block,
        jnp.concatenate([w_key, w_value], axis=1),
        pack(GROUPS[0], z_index, queries, out_grad),
        z_index,
    )
    encoder = gathered[:, :ENC_ROWS].reshape(KEYS, -1)
    all_ids = (gathered[:, ENC_ROWS, :ENC_ROWS], gathered[:, ENC_ROWS + 1, :ROWS])
    first_of = jnp.arange(1, 4, dtype=BF16)[:, None, None]
    ends = jnp.concatenate([jnp.sum((i[None] < first_of).astype(jnp.int32), axis=(1, 2)) for i in all_ids])
    swap = functools.partial(
        lax.all_to_all,
        axis_name="ctx",
        split_axis=0,
        concat_axis=0,
        axis_index_groups=SHARED_Z,
        tiled=True,
    )
    near = swap(near_packed)
    own = jnp.dot(encoder, weight, preferred_element_type=F32).astype(BF16)
    far_packed = pack(GROUPS[1], z_later, queries, out_grad)
    far_packed, near, own = lax.optimization_barrier((far_packed, near, own))
    far = swap(far_packed)

    own_key, own_value = own[:, :FEATURES], own[:, FEATURES:]
    key_ahead, value_behind = shift(own_key, dz=-1), shift(own_value, dz=1)
    back, key_0, value_0 = attend(ends, near, 0, own_key[None], own_value[None])
    key_ahead, value_behind, back = lax.optimization_barrier((key_ahead, value_behind, back))
    key_opposite, value_opposite = shift(key_ahead, dz=-1), shift(value_behind, dz=1)
    later_key, later_value, key_opposite, value_opposite = lax.optimization_barrier(
        (own_key, own_value, key_opposite, value_opposite)
    )
    key_behind, value_ahead = shift(later_key, dz=1), shift(later_value, dz=-1)

    back, key_2, value_2 = attend(ends, near, 1, key_opposite[None], value_opposite[None], back)
    back_near = swap(back)
    back, key_1, value_1 = attend(
        ends,
        far,
        0,
        jnp.stack([key_ahead, key_behind]),
        jnp.stack([value_ahead, value_behind]),
    )

    def joined(a, b):
        return (a.astype(F32) + b.astype(F32)).astype(BF16)

    key_sum = joined(key_1[0], shift(key_2[0], dz=1))
    value_sum = joined(value_1[1], shift(value_2[0], dz=-1))
    for_ahead = jnp.concatenate([key_sum, value_1[0]], axis=1)
    for_behind = jnp.concatenate([key_1[1], value_sum], axis=1)
    for_ahead, for_behind, back = lax.optimization_barrier((for_ahead, for_behind, back))
    total = jnp.concatenate([key_0[0], value_0[0]], axis=1).astype(F32)
    total += shift(for_ahead, dz=1).astype(F32) + shift(for_behind, dz=-1).astype(F32)

    query_grad = unpack(GROUPS[0], z_index, back_near)
    total, query_grad = lax.optimization_barrier((total, query_grad))
    back = swap(back)
    rounded = total.astype(BF16)
    part = lax.dot_general(rounded, weight, (((1,), (1,)), ((), ())), preferred_element_type=F32)
    part = part.astype(BF16).reshape(NY, NZ, NC, ENC_ROWS, -1)
    enc_grad, encoder, back = sum_encoder(part, encoder, back)
    query_grad = unpack(GROUPS[1], z_index, back, query_grad)

    term = lax.dot_general(encoder, rounded, (((0,), (0,)), ((), ())), preferred_element_type=F32)
    pieces = term.astype(BF16).reshape(NX * NL, -1, 2 * FEATURES)
    pieces = lax.all_to_all(pieces, "dp", 0, 0, tiled=True)
    weight_grad = pieces.astype(F32).sum(axis=0)
    return query_grad, enc_grad, weight_grad[:, :FEATURES], weight_grad[:, FEATURES:]


def solution(mesh):
    tokens, weights, ids = P(("dp", "ctx"), None), P("dp", "ctx"), P(("dp", "ctx"))
    return jax.shard_map(
        body,
        mesh=mesh,
        in_specs=(tokens, tokens, tokens, weights, weights, ids, ids),
        out_specs=(tokens, tokens, weights, weights),
        check_vma=False,
    )
```

```python
import functools
import math

import jax
import jax.numpy as jnp
from jax import lax
from jax.experimental import pallas as pl
from jax.experimental.pallas import tpu as pltpu
from jax.sharding import PartitionSpec as P

HEAD_DIM = 128
NY, NZ, NC = 4, 4, 2
NX, NL = 4, 2
PEERS = NY * NC
ROWS = 128
KEYS = 384
ENC_ROWS = 12
FEATURES = 256
SHARED_Z = [[(y * NZ + z) * NC + c for y in range(NY) for c in range(NC)] for z in range(NZ)]
GROUPS = ((1, 3), (0, 2))

BF16, F32 = jnp.bfloat16, jnp.float32


def place():
    me = lax.axis_index("ctx")
    return me >> 3, (me >> 1) & 3, me & 1


def shift(value, dy=0, dz=0, dc=0):
    pairs = [
        ((y * NZ + z) * NC + c, (((y + dy) % NY) * NZ + (z + dz) % NZ) * NC + (c + dc) % NC)
        for y in range(NY)
        for z in range(NZ)
        for c in range(NC)
    ]
    return lax.ppermute(value, "ctx", pairs)


def by_owner(mine, arrived, me):
    blocks = [mine, *arrived]
    n = len(blocks)
    if n == 2:
        first = me == 0
        return jnp.stack([jnp.where(first, *blocks), jnp.where(first, *blocks[::-1])])
    return jnp.stack([lax.select_n((owner - me) & (n - 1), *blocks) for owner in range(n)])


def double(held, bit):
    other = lax.ppermute(held, "dp", [(d, d ^ bit) for d in range(NX * NL)])
    first = (lax.axis_index("dp") & bit) == 0
    return jnp.concatenate([jnp.where(first, held, other), jnp.where(first, other, held)])


def along_x(pair):
    x = lax.axis_index("dp") >> 1

    def from_ahead(d):
        pairs = [(a * NL + b, (a - d) % NX * NL + b) for a in range(NX) for b in range(NL)]
        return lax.ppermute(pair, "dp", pairs)

    return by_owner(pair, [from_ahead(d) for d in range(1, NX)], x).reshape(-1, *pair.shape[1:])


def gather(block, weight, packed, later):
    y, z, c = place()
    weight = double(weight[None], 1)
    along_y = by_owner(block, [shift(block, dy=-d) for d in range(1, NY)], y)
    along_y, weight, packed = lax.optimization_barrier((along_y, weight, packed))
    weight = along_x(weight)
    along_z = by_owner(along_y, [shift(along_y, dz=-d) for d in range(1, NZ)], z)
    along_z, later = lax.optimization_barrier((along_z, later))
    other = shift(along_z, dc=1)
    first = c == 0
    both = [jnp.where(first, along_z, other), jnp.where(first, other, along_z)]
    gathered = jnp.stack(both, axis=2).swapaxes(0, 1)
    return gathered.reshape(NY * NZ * NC, *block.shape), weight.reshape(-1, weight.shape[2]), packed, later


def at(value, index, axis):
    start = [0] * value.ndim
    start[axis] = index
    size = [1 if i == axis else n for i, n in enumerate(value.shape)]
    return lax.dynamic_slice(value, start, size, allow_negative_indices=False).squeeze(axis)


def half_sum(part, axis, bit):
    mine = (lax.axis_index("dp") & bit) == 0
    low, high = (lax.index_in_dim(part, i, axis, keepdims=False) for i in range(2))
    other = lax.ppermute(jnp.where(mine, high, low), "dp", [(d, d ^ bit) for d in range(NX * NL)])
    return jnp.where(mine, low, high).astype(F32) + other.astype(F32)


def sums(part, encoder, rounded, returned):
    y, z, c = place()
    arrived = shift(at(part, 1 - c, 2), dc=1)
    total = (at(part, c, 2).astype(F32) + arrived.astype(F32)).astype(BF16)
    term = lax.dot_general(encoder, rounded, (((0,), (0,)), ((), ())), preferred_element_type=F32)
    term = half_sum(term.astype(BF16).reshape(2, 2, 2, -1, 2 * FEATURES), 1, 2).astype(BF16)
    total, returned = lax.optimization_barrier((total, returned))
    arrived = [shift(at(total, (y + d) & 3, 0), dy=d) for d in range(1, NY)]
    total = sum((a.astype(F32) for a in arrived), at(total, y, 0).astype(F32)).astype(BF16)
    _, term, returned = lax.optimization_barrier((total, term, returned))
    arrived = [shift(at(total, (z + d) & 3, 0), dz=d) for d in range(1, NZ)]
    enc_grad = sum((a.astype(F32) for a in arrived), at(total, z, 0).astype(F32)).astype(BF16)
    weight_grad = half_sum(half_sum(term, 0, 4).astype(BF16), 0, 1)
    return enc_grad, weight_grad, returned


def pack_kernel(z, *refs):
    sources, out = refs[:-1], refs[-1]
    for i in range(len(sources) // 2):
        for which in range(2):
            for c in range(NC):
                block = sources[2 * i + which][:, pl.ds(c * FEATURES, FEATURES)]
                out[c, which, :, pl.ds(i * FEATURES, FEATURES)] = block


def pack(group, z, queries, grads):
    shape = (2, ROWS, len(group) * FEATURES)
    columns = [
        pl.BlockSpec((ROWS, NC * FEATURES), lambda y, z, d=d: (0, y * NZ + lax.rem(z[0] + d, NZ)))
        for d in group
        for _ in range(2)
    ]
    return pl.pallas_call(
        pack_kernel,
        out_shape=jax.ShapeDtypeStruct((PEERS, *shape), BF16),
        grid_spec=pltpu.PrefetchScalarGridSpec(
            num_scalar_prefetch=1,
            grid=(NY,),
            in_specs=columns,
            out_specs=pl.BlockSpec((NC, *shape), lambda y, z: (y, 0, 0, 0)),
        ),
        cost_estimate=pl.CostEstimate(
            flops=0, bytes_accessed=4 * PEERS * math.prod(shape), transcendentals=0
        ),
    )(z, *[queries, grads] * len(group))


def unpack_kernel(z, *refs):
    sources, out = refs[:-1], refs[-1]
    for group, source in zip(GROUPS, sources, strict=True):
        for i, distance in enumerate(group):
            for c in range(NC):
                start = (lax.rem(z[0] + distance, NZ) * NC + c) * FEATURES
                columns = pl.ds(pl.multiple_of(start, FEATURES), FEATURES)
                out[:, columns] = source[c, :, pl.ds(i * FEATURES, FEATURES)]


def unpack(z, arrived):
    width = NZ * NC * FEATURES
    return pl.pallas_call(
        unpack_kernel,
        out_shape=jax.ShapeDtypeStruct((ROWS, NY * width), BF16),
        grid_spec=pltpu.PrefetchScalarGridSpec(
            num_scalar_prefetch=1,
            grid=(NY,),
            in_specs=[
                pl.BlockSpec((NC, ROWS, a.shape[2]), lambda y, z: (y, 0, 0)) for a in arrived
            ],
            out_specs=pl.BlockSpec((ROWS, width), lambda y, z: (0, y)),
        ),
        cost_estimate=pl.CostEstimate(
            flops=0, bytes_accessed=4 * ROWS * NY * width, transcendentals=0
        ),
    )(z, *arrived)


def attend_kernel(ends, rows, key, value, *refs):
    query_grad, key_grad, value_grad, bias = refs[-4:]
    tile = NC * ROWS

    @pl.when(pl.program_id(0) == 0)
    def _():
        z = lax.rem(lax.div(lax.axis_index("ctx"), NC), NZ)
        keys_at = lax.broadcasted_iota(jnp.int32, (KEYS, tile), 0)
        for y in range(NY):
            token = (y * NZ + z) * tile + lax.broadcasted_iota(jnp.int32, (1, tile), 1)
            low = jnp.zeros((1, tile), jnp.int32)
            high = jnp.full((1, tile), ends[0], jnp.int32)
            for d in range(3):
                past = token >= ends[3 + d]
                low = jnp.where(past, ends[d], low)
                high = jnp.where(past, ends[d + 1] if d < 2 else KEYS, high)
            allowed = (keys_at >= low) & (keys_at < high)
            bias[:, pl.ds(y * tile, tile)] = jnp.where(allowed, 0.0, -jnp.inf)

    keys, values = key[0], value[0]
    last, first = (((1,), (1,)), ((), ())), (((0,), (0,)), ((), ()))
    query = rows[:, 0].reshape(PEERS * ROWS, HEAD_DIM)
    grad = rows[:, 1].reshape(PEERS * ROWS, HEAD_DIM)
    scores = lax.dot_general(keys, query, last, preferred_element_type=F32) + bias[...]
    weights = jnp.exp(scores - jnp.max(scores, axis=0, keepdims=True))
    probability = weights * (1.0 / jnp.sum(weights, axis=0, keepdims=True))
    upstream = lax.dot_general(values, grad, last, preferred_element_type=F32)
    row_dot = jnp.sum(probability * upstream, axis=0, keepdims=True)
    score_grad = (probability * (upstream - row_dot)).astype(BF16)
    rounded = probability.astype(BF16)
    key_grad[0] = jnp.dot(score_grad, query, preferred_element_type=F32).astype(BF16)
    value_grad[0] = jnp.dot(rounded, grad, preferred_element_type=F32).astype(BF16)
    returned = lax.dot_general(score_grad, keys, first, preferred_element_type=F32)
    query_grad[...] = returned.astype(BF16).reshape(PEERS, ROWS, HEAD_DIM)


def attend(ends, rows, first, keys, values, into=None):
    count = keys.shape[0]
    heads = FEATURES // HEAD_DIM
    given = [] if into is None else [into]
    elements = count * heads * PEERS * ROWS * KEYS
    block = (1, KEYS, HEAD_DIM)
    in_block = lambda h, ends: (h // heads, 0, h % heads)
    grads = jax.ShapeDtypeStruct((count, KEYS, FEATURES), BF16)
    return pl.pallas_call(
        attend_kernel,
        out_shape=(jax.ShapeDtypeStruct((PEERS, ROWS, rows.shape[3]), BF16), grads, grads),
        grid_spec=pltpu.PrefetchScalarGridSpec(
            num_scalar_prefetch=1,
            grid=(count * heads,),
            in_specs=[
                pl.BlockSpec(
                    (PEERS, 2, ROWS, HEAD_DIM), lambda h, ends: (0, 0, 0, first * heads + h)
                ),
                pl.BlockSpec(block, in_block),
                pl.BlockSpec(block, in_block),
                *[pl.BlockSpec(memory_space=pl.ANY) for _ in given],
            ],
            out_specs=(
                pl.BlockSpec((PEERS, ROWS, HEAD_DIM), lambda h, ends: (0, 0, first * heads + h)),
                pl.BlockSpec(block, in_block),
                pl.BlockSpec(block, in_block),
            ),
            scratch_shapes=[pltpu.VMEM((KEYS, PEERS * ROWS), F32)],
        ),
        compiler_params=pltpu.CompilerParams(vmem_limit_bytes=24 * 2**20),
        cost_estimate=pl.CostEstimate(
            flops=elements * HEAD_DIM * 10, bytes_accessed=6 * 2**20, transcendentals=elements
        ),
        input_output_aliases={4: 0} if given else {},
    )(ends, rows, keys, values, *given)


def body(queries, out_grad, enc_states, w_key, w_value, dec_segments, enc_segments):
    z = place()[1]
    z_index = z.reshape(1)
    width = enc_states.shape[1]
    ids = [jnp.pad(i.astype(BF16)[None], ((0, 0), (0, width - i.size))) for i in (enc_segments, dec_segments)]
    block = jnp.concatenate([enc_states, *ids, jnp.zeros((2, width), BF16)], axis=0)
    gathered, weight, near_packed, z_later = gather(
        block,
        jnp.concatenate([w_key, w_value], axis=1),
        pack(GROUPS[0], z_index, queries, out_grad),
        z_index,
    )
    encoder = gathered[:, :ENC_ROWS].reshape(KEYS, -1)
    all_ids = (gathered[:, ENC_ROWS, :ENC_ROWS], gathered[:, ENC_ROWS + 1, :ROWS])
    first_of = jnp.arange(1, 4, dtype=BF16)[:, None, None]
    ends = jnp.concatenate([jnp.sum((i[None] < first_of).astype(jnp.int32), axis=(1, 2)) for i in all_ids])
    swap = functools.partial(
        lax.all_to_all,
        axis_name="ctx",
        split_axis=0,
        concat_axis=0,
        axis_index_groups=SHARED_Z,
        tiled=True,
    )
    near = swap(near_packed)
    own = jnp.dot(encoder, weight, preferred_element_type=F32).astype(BF16)
    far_packed = pack(GROUPS[1], z_later, queries, out_grad)
    far_packed, near, own = lax.optimization_barrier((far_packed, near, own))
    far = swap(far_packed)

    own_key, own_value = own[:, :FEATURES], own[:, FEATURES:]
    ahead, behind = shift(own, dz=-1), shift(own, dz=1)
    key_ahead, value_ahead = ahead[:, :FEATURES], ahead[:, FEATURES:]
    key_behind, value_behind = behind[:, :FEATURES], behind[:, FEATURES:]
    key_opposite, value_opposite = shift(key_ahead, dz=-1), shift(value_behind, dz=1)

    back_near, key_1, value_1 = attend(
        ends,
        near,
        0,
        jnp.stack([key_ahead, key_behind]),
        jnp.stack([value_ahead, value_behind]),
    )
    key_opposite, value_opposite, key_1, value_1 = lax.optimization_barrier(
        (key_opposite, value_opposite, key_1, value_1)
    )
    value_part, key_part = shift(value_1[0], dz=1), shift(key_1[1], dz=-1)
    back, key_2, value_2 = attend(ends, far, 1, key_opposite[None], value_opposite[None])
    key_2, value_2, own_key, own_value = lax.optimization_barrier(
        (key_2, value_2, own_key, own_value)
    )
    key_sum, value_sum = shift(key_2[0], dz=1), shift(value_2[0], dz=-1)
    back, key_0, value_0 = attend(ends, far, 0, own_key[None], own_value[None], back)
    back_near = swap(back_near)
    key_sum, value_sum, key_part, value_part, key_0, value_0, back, back_near = (
        lax.optimization_barrier(
            (key_sum, value_sum, key_part, value_part, key_0, value_0, back, back_near)
        )
    )

    def joined(a, b):
        return (a.astype(F32) + b.astype(F32)).astype(BF16)

    key_sum, value_sum = joined(key_1[0], key_sum), joined(value_1[1], value_sum)
    own_terms = jnp.concatenate([key_0[0], value_0[0]], axis=1).astype(F32)
    own_terms += jnp.concatenate([key_part, value_part], axis=1).astype(F32)
    arrived = jnp.concatenate([shift(key_sum, dz=1), shift(value_sum, dz=-1)], axis=1)
    rounded = (own_terms + arrived.astype(F32)).astype(BF16)
    back_far = swap(back)

    part = lax.dot_general(rounded, weight, (((1,), (1,)), ((), ())), preferred_element_type=F32)
    part = part.astype(BF16).reshape(NY, NZ, NC, ENC_ROWS, -1)
    enc_grad, weight_grad, returned = sums(part, encoder, rounded, [back_near, back_far])
    query_grad = unpack(z_index, returned)
    return query_grad, enc_grad, weight_grad[:, :FEATURES], weight_grad[:, FEATURES:]


def solution(mesh):
    tokens, weights, ids = P(("dp", "ctx"), None), P("dp", "ctx"), P(("dp", "ctx"))
    return jax.shard_map(
        body,
        mesh=mesh,
        in_specs=(tokens, tokens, tokens, weights, weights, ids, ids),
        out_specs=(tokens, tokens, weights, weights),
        check_vma=False,
    )
```

```python
import functools
import math

import jax
import jax.numpy as jnp
from jax import lax
from jax.experimental import pallas as pl
from jax.experimental.pallas import tpu as pltpu
from jax.sharding import PartitionSpec as P

HEAD_DIM = 128
NY, NZ, NC = 4, 4, 2
NX, NL = 4, 2
PEERS = NY * NC
ROWS = 128
KEYS = 384
ENC_ROWS = 12
FEATURES = 256
SHARED_Z = [[(y * NZ + z) * NC + c for y in range(NY) for c in range(NC)] for z in range(NZ)]
GROUPS = ((1, 3), (0, 2))

BF16, F32 = jnp.bfloat16, jnp.float32


def place():
    me = lax.axis_index("ctx")
    return me >> 3, (me >> 1) & 3, me & 1


def shift(value, dy=0, dz=0, dc=0):
    pairs = [
        ((y * NZ + z) * NC + c, (((y + dy) % NY) * NZ + (z + dz) % NZ) * NC + (c + dc) % NC)
        for y in range(NY)
        for z in range(NZ)
        for c in range(NC)
    ]
    return lax.ppermute(value, "ctx", pairs)


def by_owner(mine, arrived, me):
    blocks = [mine, *arrived]
    n = len(blocks)
    if n == 2:
        first = me == 0
        return jnp.stack([jnp.where(first, *blocks), jnp.where(first, *blocks[::-1])])
    return jnp.stack([lax.select_n((owner - me) & (n - 1), *blocks) for owner in range(n)])


def double(held, bit):
    other = lax.ppermute(held, "dp", [(d, d ^ bit) for d in range(NX * NL)])
    first = (lax.axis_index("dp") & bit) == 0
    return jnp.concatenate([jnp.where(first, held, other), jnp.where(first, other, held)])


def along_x(pair):
    x = lax.axis_index("dp") >> 1

    def from_ahead(d):
        pairs = [(a * NL + b, (a - d) % NX * NL + b) for a in range(NX) for b in range(NL)]
        return lax.ppermute(pair, "dp", pairs)

    return by_owner(pair, [from_ahead(d) for d in range(1, NX)], x).reshape(-1, *pair.shape[1:])


def gather(block, weight, packed, later):
    y, z, c = place()
    weight = double(weight[None], 1)
    along_y = by_owner(block, [shift(block, dy=-d) for d in range(1, NY)], y)
    along_y, weight, packed = lax.optimization_barrier((along_y, weight, packed))
    weight = along_x(weight)
    along_z = by_owner(along_y, [shift(along_y, dz=-d) for d in range(1, NZ)], z)
    along_z, later = lax.optimization_barrier((along_z, later))
    other = shift(along_z, dc=1)
    first = c == 0
    both = [jnp.where(first, along_z, other), jnp.where(first, other, along_z)]
    gathered = jnp.stack(both, axis=2).swapaxes(0, 1)
    return gathered.reshape(NY * NZ * NC, *block.shape), weight.reshape(-1, weight.shape[2]), packed, later


def at(value, index, axis):
    start = [0] * value.ndim
    start[axis] = index
    size = [1 if i == axis else n for i, n in enumerate(value.shape)]
    return lax.dynamic_slice(value, start, size, allow_negative_indices=False).squeeze(axis)


def half_sum(part, axis, bit):
    mine = (lax.axis_index("dp") & bit) == 0
    low, high = (lax.index_in_dim(part, i, axis, keepdims=False) for i in range(2))
    other = lax.ppermute(jnp.where(mine, high, low), "dp", [(d, d ^ bit) for d in range(NX * NL)])
    return jnp.where(mine, low, high).astype(F32) + other.astype(F32)


def sums(part, encoder, rounded, returned):
    y, z, c = place()
    arrived = shift(at(part, 1 - c, 2), dc=1)
    total = (at(part, c, 2).astype(F32) + arrived.astype(F32)).astype(BF16)
    term = lax.dot_general(encoder, rounded, (((0,), (0,)), ((), ())), preferred_element_type=F32)
    term = half_sum(term.astype(BF16).reshape(2, 2, 2, -1, 2 * FEATURES), 1, 2).astype(BF16)
    total, returned = lax.optimization_barrier((total, returned))
    arrived = [shift(at(total, (y + d) & 3, 0), dy=d) for d in range(1, NY)]
    total = sum((a.astype(F32) for a in arrived), at(total, y, 0).astype(F32)).astype(BF16)
    _, term, returned = lax.optimization_barrier((total, term, returned))
    arrived = [shift(at(total, (z + d) & 3, 0), dz=d) for d in range(1, NZ)]
    enc_grad = sum((a.astype(F32) for a in arrived), at(total, z, 0).astype(F32)).astype(BF16)
    weight_grad = half_sum(half_sum(term, 0, 4).astype(BF16), 0, 1)
    return enc_grad, weight_grad, returned


def pack_kernel(z, *refs):
    sources, out = refs[:-1], refs[-1]
    for i in range(len(sources) // 2):
        for which in range(2):
            for c in range(NC):
                block = sources[2 * i + which][:, pl.ds(c * FEATURES, FEATURES)]
                out[c, which, :, pl.ds(i * FEATURES, FEATURES)] = block


def pack(group, z, queries, grads):
    shape = (2, ROWS, len(group) * FEATURES)
    columns = [
        pl.BlockSpec((ROWS, NC * FEATURES), lambda y, z, d=d: (0, y * NZ + lax.rem(z[0] + d, NZ)))
        for d in group
        for _ in range(2)
    ]
    return pl.pallas_call(
        pack_kernel,
        out_shape=jax.ShapeDtypeStruct((PEERS, *shape), BF16),
        grid_spec=pltpu.PrefetchScalarGridSpec(
            num_scalar_prefetch=1,
            grid=(NY,),
            in_specs=columns,
            out_specs=pl.BlockSpec((NC, *shape), lambda y, z: (y, 0, 0, 0)),
        ),
        cost_estimate=pl.CostEstimate(
            flops=0, bytes_accessed=4 * PEERS * math.prod(shape), transcendentals=0
        ),
    )(z, *[queries, grads] * len(group))


def unpack_kernel(z, *refs):
    sources, out = refs[:-1], refs[-1]
    for group, source in zip(GROUPS, sources, strict=True):
        for i, distance in enumerate(group):
            for c in range(NC):
                start = (lax.rem(z[0] + distance, NZ) * NC + c) * FEATURES
                columns = pl.ds(pl.multiple_of(start, FEATURES), FEATURES)
                out[:, columns] = source[c, :, pl.ds(i * FEATURES, FEATURES)]


def unpack(z, arrived):
    width = NZ * NC * FEATURES
    return pl.pallas_call(
        unpack_kernel,
        out_shape=jax.ShapeDtypeStruct((ROWS, NY * width), BF16),
        grid_spec=pltpu.PrefetchScalarGridSpec(
            num_scalar_prefetch=1,
            grid=(NY,),
            in_specs=[
                pl.BlockSpec((NC, ROWS, a.shape[2]), lambda y, z: (y, 0, 0)) for a in arrived
            ],
            out_specs=pl.BlockSpec((ROWS, width), lambda y, z: (0, y)),
        ),
        cost_estimate=pl.CostEstimate(
            flops=0, bytes_accessed=4 * ROWS * NY * width, transcendentals=0
        ),
    )(z, *arrived)


def attend_kernel(ends, rows, key, value, *refs):
    query_grad, key_grad, value_grad, bias = refs[-4:]
    tile = NC * ROWS

    @pl.when(pl.program_id(0) == 0)
    def _():
        z = lax.rem(lax.div(lax.axis_index("ctx"), NC), NZ)
        keys_at = lax.broadcasted_iota(jnp.int32, (KEYS, tile), 0)
        for y in range(NY):
            token = (y * NZ + z) * tile + lax.broadcasted_iota(jnp.int32, (1, tile), 1)
            low = jnp.zeros((1, tile), jnp.int32)
            high = jnp.full((1, tile), ends[0], jnp.int32)
            for d in range(3):
                past = token >= ends[3 + d]
                low = jnp.where(past, ends[d], low)
                high = jnp.where(past, ends[d + 1] if d < 2 else KEYS, high)
            allowed = (keys_at >= low) & (keys_at < high)
            bias[:, pl.ds(y * tile, tile)] = jnp.where(allowed, 0.0, -jnp.inf)

    keys, values = key[0], value[0]
    last, first = (((1,), (1,)), ((), ())), (((0,), (0,)), ((), ()))
    query = rows[:, 0].reshape(PEERS * ROWS, HEAD_DIM)
    grad = rows[:, 1].reshape(PEERS * ROWS, HEAD_DIM)
    scores = lax.dot_general(keys, query, last, preferred_element_type=F32) + bias[...]
    weights = jnp.exp(scores - jnp.max(scores, axis=0, keepdims=True))
    probability = weights * (1.0 / jnp.sum(weights, axis=0, keepdims=True))
    upstream = lax.dot_general(values, grad, last, preferred_element_type=F32)
    row_dot = jnp.sum(probability * upstream, axis=0, keepdims=True)
    score_grad = (probability * (upstream - row_dot)).astype(BF16)
    rounded = probability.astype(BF16)
    key_grad[0] = jnp.dot(score_grad, query, preferred_element_type=F32).astype(BF16)
    value_grad[0] = jnp.dot(rounded, grad, preferred_element_type=F32).astype(BF16)
    returned = lax.dot_general(score_grad, keys, first, preferred_element_type=F32)
    query_grad[...] = returned.astype(BF16).reshape(PEERS, ROWS, HEAD_DIM)


def attend(ends, rows, first, keys, values, into=None):
    count = keys.shape[0]
    heads = FEATURES // HEAD_DIM
    given = [] if into is None else [into]
    elements = count * heads * PEERS * ROWS * KEYS
    block = (1, KEYS, HEAD_DIM)
    in_block = lambda h, ends: (h // heads, 0, h % heads)
    grads = jax.ShapeDtypeStruct((count, KEYS, FEATURES), BF16)
    return pl.pallas_call(
        attend_kernel,
        out_shape=(jax.ShapeDtypeStruct((PEERS, ROWS, rows.shape[3]), BF16), grads, grads),
        grid_spec=pltpu.PrefetchScalarGridSpec(
            num_scalar_prefetch=1,
            grid=(count * heads,),
            in_specs=[
                pl.BlockSpec(
                    (PEERS, 2, ROWS, HEAD_DIM), lambda h, ends: (0, 0, 0, first * heads + h)
                ),
                pl.BlockSpec(block, in_block),
                pl.BlockSpec(block, in_block),
                *[pl.BlockSpec(memory_space=pl.ANY) for _ in given],
            ],
            out_specs=(
                pl.BlockSpec((PEERS, ROWS, HEAD_DIM), lambda h, ends: (0, 0, first * heads + h)),
                pl.BlockSpec(block, in_block),
                pl.BlockSpec(block, in_block),
            ),
            scratch_shapes=[pltpu.VMEM((KEYS, PEERS * ROWS), F32)],
        ),
        compiler_params=pltpu.CompilerParams(vmem_limit_bytes=24 * 2**20),
        cost_estimate=pl.CostEstimate(
            flops=elements * HEAD_DIM * 10, bytes_accessed=6 * 2**20, transcendentals=elements
        ),
        input_output_aliases={4: 0} if given else {},
    )(ends, rows, keys, values, *given)


def body(queries, out_grad, enc_states, w_key, w_value, dec_segments, enc_segments):
    z = place()[1]
    z_index = z.reshape(1)
    width = enc_states.shape[1]
    ids = [jnp.pad(i.astype(BF16)[None], ((0, 0), (0, width - i.size))) for i in (enc_segments, dec_segments)]
    block = jnp.concatenate([enc_states, *ids, jnp.zeros((2, width), BF16)], axis=0)
    gathered, weight, near_packed, z_later = gather(
        block,
        jnp.concatenate([w_key, w_value], axis=1),
        pack(GROUPS[0], z_index, queries, out_grad),
        z_index,
    )
    encoder = gathered[:, :ENC_ROWS].reshape(KEYS, -1)
    all_ids = (gathered[:, ENC_ROWS, :ENC_ROWS], gathered[:, ENC_ROWS + 1, :ROWS])
    first_of = jnp.arange(1, 4, dtype=BF16)[:, None, None]
    ends = jnp.concatenate([jnp.sum((i[None] < first_of).astype(jnp.int32), axis=(1, 2)) for i in all_ids])
    swap = functools.partial(
        lax.all_to_all,
        axis_name="ctx",
        split_axis=0,
        concat_axis=0,
        axis_index_groups=SHARED_Z,
        tiled=True,
    )
    near = swap(near_packed)
    own = jnp.dot(encoder, weight, preferred_element_type=F32).astype(BF16)
    far_packed = pack(GROUPS[1], z_later, queries, out_grad)
    far_packed, near = lax.optimization_barrier((far_packed, near))
    far = swap(far_packed)

    own_key, own_value = own[:, :FEATURES], own[:, FEATURES:]
    ahead, behind = shift(own, dz=-1), shift(own, dz=1)
    key_ahead, value_ahead = ahead[:, :FEATURES], ahead[:, FEATURES:]
    key_behind, value_behind = behind[:, :FEATURES], behind[:, FEATURES:]
    key_opposite, value_opposite = shift(key_ahead, dz=-1), shift(value_behind, dz=1)

    back_near, key_1, value_1 = attend(
        ends,
        near,
        0,
        jnp.stack([key_ahead, key_behind]),
        jnp.stack([value_ahead, value_behind]),
    )
    key_opposite, value_opposite, key_1, value_1 = lax.optimization_barrier(
        (key_opposite, value_opposite, key_1, value_1)
    )
    value_part, key_part = shift(value_1[0], dz=1), shift(key_1[1], dz=-1)
    back, key_2, value_2 = attend(ends, far, 1, key_opposite[None], value_opposite[None])
    key_2, value_2, own_key, own_value = lax.optimization_barrier(
        (key_2, value_2, own_key, own_value)
    )
    key_sum, value_sum = shift(key_2[0], dz=1), shift(value_2[0], dz=-1)
    back, key_0, value_0 = attend(ends, far, 0, own_key[None], own_value[None], back)
    back_near = swap(back_near)
    key_sum, value_sum, key_part, value_part, key_0, value_0, back, back_near = (
        lax.optimization_barrier(
            (key_sum, value_sum, key_part, value_part, key_0, value_0, back, back_near)
        )
    )

    def joined(a, b):
        return (a.astype(F32) + b.astype(F32)).astype(BF16)

    key_sum, value_sum = joined(key_1[0], key_sum), joined(value_1[1], value_sum)
    own_terms = jnp.concatenate([key_0[0], value_0[0]], axis=1).astype(F32)
    own_terms += jnp.concatenate([key_part, value_part], axis=1).astype(F32)
    arrived = jnp.concatenate([shift(key_sum, dz=1), shift(value_sum, dz=-1)], axis=1)
    rounded = (own_terms + arrived.astype(F32)).astype(BF16)
    back_far = swap(back)

    part = lax.dot_general(rounded, weight, (((1,), (1,)), ((), ())), preferred_element_type=F32)
    part = part.astype(BF16).reshape(NY, NZ, NC, ENC_ROWS, -1)
    enc_grad, weight_grad, returned = sums(part, encoder, rounded, [back_near, back_far])
    query_grad = unpack(z_index, returned)
    return query_grad, enc_grad, weight_grad[:, :FEATURES], weight_grad[:, FEATURES:]


def solution(mesh):
    tokens, weights, ids = P(("dp", "ctx"), None), P("dp", "ctx"), P(("dp", "ctx"))
    return jax.shard_map(
        body,
        mesh=mesh,
        in_specs=(tokens, tokens, tokens, weights, weights, ids, ids),
        out_specs=(tokens, tokens, weights, weights),
        check_vma=False,
    )
```
